32 devices in a mesh: grp: 2 (over y), tile: 8 (over z, x), tm: 2 (over core).
Axes of the slice: x: 2, y: 2, z: 4, core: 2. Of those that a mesh axis runs over, the one named last changes fastest.
Arguments:
- video: bfloat16 [8, 16, 256, 128], P(('grp', 'tm'), 'tile'), parts along dimension 0, may hold values from -60 to 60
- conv_first: bfloat16 [3, 3, 3, 128, 128], replicated, may hold values from -0.109375 to 0.109375
- conv_second: bfloat16 [3, 3, 3, 128, 128], replicated, may hold values from -0.109375 to 0.109375
- gain_first: float32 [128], replicated, may hold values from 0.1 to 1.9
- shift_first: float32 [128], replicated, may hold values from -3 to 3
- gain_second: float32 [128], replicated, may hold values from 0.1 to 1.9
- shift_second: float32 [128], replicated, may hold values from -3 to 3
- bias_second: float32 [128], replicated, may hold values from -3 to 3
Outputs:
- encoded: bfloat16 [8, 16, 256, 128], P(('grp', 'tm'), 'tile'), parts along dimension 0
The draws below stay inside these ranges and needn't reach their ends.
There are 2 independent parts, one for each index of `grp`. The reference program is written for one: setup_inputs(seed, part) draws one part's arguments, and reference() takes and returns one part's arrays. A program takes and returns all parts, laid end to end along the dimension named above; an argument that names none is the same for every part. Nothing has to cross between parts.
All inputs are finite; a program needn't handle non-finite values.
Results may differ from the reference program's by a relative error of at most 0.002.
Values may be sent and summed in bfloat16 or wider, within the bound.
A program may use at most 64 MiB of HBM per device.

```python
import math
import jax
import jax.numpy as jnp
from jax import lax

C = 128
G = 32
COLS = 256
FRAMES = 4
HEIGHT = 16


def draw_video(key, part):
    key_list = jax.random.split(key, 9)
    base_draw = jax.random.normal(key_list[0], (FRAMES, HEIGHT, COLS, C), jnp.float32)
    row_factor = jnp.exp(jax.random.uniform(key_list[6], (HEIGHT,), jnp.float32, math.log(0.3), math.log(3.0)))
    row_offset = 1.5 * jax.random.normal(key_list[7], (HEIGHT,), jnp.float32)
    frame_factor = jnp.exp(jax.random.uniform(key_list[8], (FRAMES,), jnp.float32, math.log(0.5), math.log(2.0)))
    col_scale = jnp.exp(jax.random.uniform(key_list[1], (COLS,), jnp.float32, 0.0, math.log(2.0)))
    chan_scale = jnp.exp(jax.random.uniform(key_list[2], (C,), jnp.float32, math.log(0.7), math.log(1.4)))
    chan_mean = 0.5 * jax.random.normal(key_list[3], (C,), jnp.float32)
    values = base_draw * chan_scale + chan_mean + row_offset[None, :, None, None]
    values = values * col_scale[None, None, :, None] * row_factor[None, :, None, None]
    values = values * frame_factor[:, None, None, None]
    return jnp.clip(values, -60.0, 60.0).astype(jnp.bfloat16)


def normal_values(rng, shape, width, reach, held_as=jnp.bfloat16):
    array = width * jax.random.normal(rng, shape, jnp.float32)
    return jnp.clip(array, min=-reach, max=reach).astype(held_as)


def setup_inputs(seed: int = 0, part: int = 0) -> dict:
    seeds = jax.random.split(jax.random.key(seed), 9)
    part_splits = jax.random.split(jax.random.fold_in(seeds[8], part), 9)
    return {
        "video": draw_video(jax.random.fold_in(jax.random.fold_in(seeds[8], part), 71), part),
        "conv_first": normal_values(seeds[1], (3, 3, 3, C, C), (27 * C) ** -0.5, 0.109375),
        "conv_second": normal_values(seeds[2], (3, 3, 3, C, C), (27 * C) ** -0.5, 0.109375),
        "gain_first": jnp.clip(1.0 + 0.18 * jax.random.normal(seeds[3], (C,), jnp.float32), 0.1, 1.9),
        "shift_first": normal_values(seeds[4], (C,), 0.5, 3.0, jnp.float32),
        "gain_second": jnp.clip(1.0 + 0.18 * jax.random.normal(seeds[5], (C,), jnp.float32), 0.1, 1.9),
        "shift_second": normal_values(seeds[6], (C,), 0.5, 3.0, jnp.float32),
        "bias_second": normal_values(seeds[7], (C,), 0.5, 3.0, jnp.float32),
    }


EPSILON = 1e-06

def group_norm(values, gain, offset):
    frame_count, row_count, col_count, channels = values.shape
    grouped = values.reshape(frame_count, row_count, col_count, G, channels // G)
    center_mean = lax.optimization_barrier(jnp.mean(grouped, axis=(0, 1, 2, 4), keepdims=True))
    deviation = grouped - center_mean
    spread = lax.optimization_barrier(jnp.mean(deviation * deviation, axis=(0, 1, 2, 4), keepdims=True))
    normed = (deviation * lax.rsqrt(spread + EPSILON)).reshape(values.shape) * gain + offset
    return jax.nn.silu(normed).astype(jnp.bfloat16)

def conv_causal(hidden, weight):
    padded = jnp.concatenate([hidden[:1], hidden[:1], hidden], axis=0).astype(jnp.float32)
    result = lax.conv_general_dilated(padded[None], weight.astype(jnp.float32), (1, 1, 1), ((0, 0), (1, 1), (1, 1)), dimension_numbers=('NDHWC', 'DHWIO', 'NDHWC'), precision=lax.Precision.HIGHEST)
    return result[0]

def reference(video, conv_first, conv_second, gain_first, shift_first, gain_second, shift_second, bias_second):
    source = video.astype(jnp.float32)
    hidden_first = group_norm(source, gain_first, shift_first)
    first_out = conv_causal(hidden_first, conv_first)
    hidden_second = group_norm(first_out, gain_second, shift_second)
    branch = conv_causal(hidden_second, conv_second)
    return (source + branch + bias_second).astype(jnp.bfloat16)
```

```python
import functools

import jax
import jax.numpy as jnp
from jax import lax
from jax.experimental import pallas as pl
from jax.experimental.pallas import tpu as pltpu
from jax.sharding import PartitionSpec as P

G = 32
EPSILON = 1e-06
MESH = pl.DeviceIdType.MESH


def group_sums(x, width):
    lanes = x.shape[-1]
    lane = lax.broadcasted_iota(jnp.int32, x.shape, 1)
    step = 1
    while step < width:
        odd = (lane // step) % 2 == 1
        x = x + jnp.where(odd, pltpu.roll(x, step, 1), pltpu.roll(x, lanes - step, 1))
        step *= 2
    return x


def kernel(
    tiles,
    video,
    conv_first,
    conv_second,
    gain_first,
    shift_first,
    gain_second,
    shift_second,
    bias_second,
    out,
    raw,
    hid,
    taps,
    weight_first,
    weight_second,
    first_out,
    result,
    stat_mine,
    stat_got,
    local_sem,
    send_sem,
    recv_sem,
):
    count = tiles * 2
    tile, tm = lax.axis_index("tile"), lax.axis_index("tm")
    me = tile * 2 + tm
    cols, chans = raw.shape[2], raw.shape[3]
    cells = float(count * 4 * cols * (chans // G))
    has_up, has_down = tile > 0, tile < tiles - 1

    load_video = pltpu.make_async_copy(video, raw.at[pl.ds(2, 2), pl.ds(0, 2)], local_sem.at[0])
    load_first = pltpu.make_async_copy(conv_first, weight_first, local_sem.at[1])
    load_second = pltpu.make_async_copy(conv_second, weight_second, local_sem.at[2])
    load_video.start()
    load_first.start()
    load_second.start()

    def peer(k):
        other = lax.rem(me + k, count)
        return {"tile": other // 2, "tm": other % 2}

    barrier = pltpu.get_barrier_semaphore()

    @pl.loop(1, count)
    def _(k):
        pl.semaphore_signal(barrier, inc=1, device_id=peer(k), device_id_type=MESH)

    @pl.when(jnp.logical_not(has_up))
    def _():
        raw[:, 2] = jnp.zeros((4, cols, chans), jnp.bfloat16)
        hid[:, 2] = jnp.zeros((4, cols, chans), jnp.bfloat16)

    @pl.when(jnp.logical_not(has_down))
    def _():
        raw[:, 3] = jnp.zeros((4, cols, chans), jnp.bfloat16)
        hid[:, 3] = jnp.zeros((4, cols, chans), jnp.bfloat16)

    load_video.wait()

    def put_stats(phase, sums, squares):
        row = lax.broadcasted_iota(jnp.int32, (8, chans), 0)
        stat_mine[phase] = jnp.where(row == 0, sums, jnp.where(row == 1, squares, 0.0))

    def send_stats(phase):
        @pl.loop(1, count)
        def _(k):
            pltpu.make_async_remote_copy(
                src_ref=stat_mine.at[phase],
                dst_ref=stat_got.at[phase, k - 1],
                send_sem=send_sem.at[phase, 5],
                recv_sem=recv_sem.at[phase, 5],
                device_id=peer(k),
                device_id_type=MESH,
            ).start()

    def get_stats(phase, gain):
        got = stat_got.at[phase]
        pltpu.make_async_copy(got, got, recv_sem.at[phase, 5]).wait()
        total = group_sums(stat_mine[phase] + jnp.sum(stat_got[phase], axis=0), chans // G)
        mean = total[0:1] / cells
        spread = total[1:2] / cells - mean * mean
        return mean, lax.rsqrt(spread + EPSILON) * gain

    def copy_of(buf, phase, which):
        own = pl.ds(2, 2)
        src, dst, device = {
            "up": (buf.at[own, 0], buf.at[own, 3], {"tile": tile - 1, "tm": tm}),
            "down": (buf.at[own, 1], buf.at[own, 2], {"tile": tile + 1, "tm": tm}),
            "mate": (
                buf.at[own, pl.ds(0, 2)],
                buf.at[pl.ds(0, 2), pl.ds(0, 2)],
                {"tile": tile, "tm": 1 - tm},
            ),
            "mate_top": (buf.at[own, 2], buf.at[pl.ds(0, 2), 2], {"tile": tile, "tm": 1 - tm}),
            "mate_bottom": (buf.at[own, 3], buf.at[pl.ds(0, 2), 3], {"tile": tile, "tm": 1 - tm}),
        }[which]
        at = ("up", "down", "mate", "mate_top", "mate_bottom").index(which)
        return pltpu.make_async_remote_copy(
            src_ref=src,
            dst_ref=dst,
            send_sem=send_sem.at[phase, at],
            recv_sem=recv_sem.at[phase, at],
            device_id=device,
            device_id_type=MESH,
        )

    def send_edges(buf, phase):
        @pl.when(has_up)
        def _():
            copy_of(buf, phase, "up").start()

        @pl.when(has_down)
        def _():
            copy_of(buf, phase, "down").start()

        @pl.when(tm == 0)
        def _():
            copy_of(buf, phase, "mate").start()

    def wait_mate(buf, phase):
        @pl.when(tm == 1)
        def _():
            copy_of(buf, phase, "mate").wait_recv()

    def wait_edges(buf, phase):
        @pl.when(has_up)
        def _():
            copy_of(buf, phase, "down").wait_recv()

        @pl.when(tm == 0)
        def _():
            copy_of(buf, phase, "mate_top").start()

        @pl.when(has_down)
        def _():
            copy_of(buf, phase, "up").wait_recv()

        @pl.when(tm == 0)
        def _():
            copy_of(buf, phase, "mate_bottom").start()

    def wait_mate_edges(buf, phase):
        @pl.when(tm == 1)
        def _():
            copy_of(buf, phase, "mate_top").wait_recv()
            copy_of(buf, phase, "mate_bottom").wait_recv()

    def wait_sends(buf, phase):
        got = stat_got.at[phase]
        pltpu.make_async_copy(got, got, send_sem.at[phase, 5]).wait()

        @pl.when(has_up)
        def _():
            copy_of(buf, phase, "up").wait_send()

        @pl.when(has_down)
        def _():
            copy_of(buf, phase, "down").wait_send()

        @pl.when(tm == 0)
        def _():
            copy_of(buf, phase, "mate").wait_send()
            copy_of(buf, phase, "mate_top").wait_send()
            copy_of(buf, phase, "mate_bottom").wait_send()

    def normalized(values, mean, scale, shift):
        normed = (values - mean) * scale + shift
        return normed * (0.5 + 0.5 * jnp.tanh(0.5 * normed))

    row = lax.broadcasted_iota(jnp.int32, (cols, chans), 0)

    def put_taps(frame, slot, h):
        before = jnp.where(row == 0, 0.0, pltpu.roll(h, 1, 0))
        after = jnp.where(row == cols - 1, 0.0, pltpu.roll(h, cols - 1, 0))
        rows, base = pl.ds(frame * cols, cols), slot * 3 * chans
        taps[rows, base : base + chans] = before.astype(jnp.bfloat16)
        taps[rows, base + chans : base + 2 * chans] = h.astype(jnp.bfloat16)
        taps[rows, base + 2 * chans : base + 3 * chans] = after.astype(jnp.bfloat16)

    wide = 3 * chans
    none = jnp.zeros((wide, chans), jnp.bfloat16)

    def conv_part(weight, part):
        total = None
        for a in range(3):
            w = weight.at[a]
            if part == 0:
                kernel_a = jnp.concatenate([w[wide : 3 * wide], w[0 : 2 * wide]], axis=1)
            else:
                kernel_a = jnp.concatenate(
                    [
                        jnp.concatenate([w[0:wide], none], axis=0),
                        jnp.concatenate([none, w[2 * wide : 3 * wide]], axis=0),
                    ],
                    axis=1,
                )
            x = taps[a * cols : (a + 2) * cols, part * 2 * wide : (part + 1) * 2 * wide]
            y = jnp.dot(x, kernel_a, preferred_element_type=jnp.float32)
            total = y if total is None else total + y
        return total

    own = [(f, s) for f in (2, 3) for s in (0, 1)]
    past = [(f, s) for f in (0, 1) for s in (0, 1)]

    def source_frame(f):
        return jnp.where(tm == 0, 2, f) if f < 2 else f

    sums = jnp.zeros((1, chans), jnp.float32)
    squares = jnp.zeros((1, chans), jnp.float32)
    for f, s in own:
        values = raw[f, s].astype(jnp.float32)
        sums = sums + jnp.sum(values, axis=0, keepdims=True)
        squares = squares + jnp.sum(values * values, axis=0, keepdims=True)
    put_stats(0, sums, squares)
    pl.semaphore_wait(barrier, count - 1)
    send_stats(0)
    send_edges(raw, 0)

    mean, scale = get_stats(0, gain_first[...])
    shift = shift_first[...]

    def first_hidden(f, s):
        h = normalized(raw[source_frame(f), s].astype(jnp.float32), mean, scale, shift)
        if s == 2:
            h = jnp.where(has_up, h, 0.0)
        if s == 3:
            h = jnp.where(has_down, h, 0.0)
        put_taps(f, s, h)

    for f, s in own:
        first_hidden(f, s)
    wait_mate(raw, 0)
    for f, s in past:
        first_hidden(f, s)
    load_first.wait()
    first_out[...] = conv_part(weight_first, 0)
    wait_edges(raw, 0)
    for f in (2, 3):
        for s in (2, 3):
            first_hidden(f, s)
    wait_mate_edges(raw, 0)
    for f in (0, 1):
        for s in (2, 3):
            first_hidden(f, s)
    first = first_out[...] + conv_part(weight_first, 1)
    first_out[...] = first

    sums = jnp.sum(first, axis=0, keepdims=True)
    squares = jnp.sum(first * first, axis=0, keepdims=True)
    put_stats(1, sums[:, :chans] + sums[:, chans:], squares[:, :chans] + squares[:, chans:])
    send_stats(1)
    mean, scale = get_stats(1, gain_second[...])
    shift = shift_second[...]
    for f, s in own:
        h = normalized(
            first_out[(f - 2) * cols : (f - 1) * cols, s * chans : (s + 1) * chans],
            mean,
            scale,
            shift,
        )
        hid[f, s] = h.astype(jnp.bfloat16)
    send_edges(hid, 1)

    def second_hidden(f, s):
        put_taps(f, s, hid[source_frame(f), s].astype(jnp.float32))

    for f, s in own:
        second_hidden(f, s)
    wait_mate(hid, 1)
    for f, s in past:
        second_hidden(f, s)
    load_second.wait()
    first_out[...] = conv_part(weight_second, 0)
    wait_edges(hid, 1)
    for f in (2, 3):
        for s in (2, 3):
            second_hidden(f, s)
    wait_mate_edges(hid, 1)
    for f in (0, 1):
        for s in (2, 3):
            second_hidden(f, s)
    branch = first_out[...] + conv_part(weight_second, 1)
    bias = bias_second[...]
    for f, s in own:
        value = branch[(f - 2) * cols : (f - 1) * cols, s * chans : (s + 1) * chans]
        result[f - 2, s] = (raw[f, s].astype(jnp.float32) + value + bias).astype(jnp.bfloat16)
    store = pltpu.make_async_copy(result, out, local_sem.at[3])
    store.start()
    wait_sends(raw, 0)
    wait_sends(hid, 1)
    store.wait()


def solution(mesh):
    tiles = mesh.shape["tile"]
    count = tiles * mesh.shape["tm"]

    def step(video, conv_first, conv_second, *vectors):
        frames, rows, cols, chans = video.shape
        any_spec = pl.BlockSpec(memory_space=pl.ANY)
        vmem_spec = pl.BlockSpec(memory_space=pltpu.VMEM)
        bf16, f32 = jnp.bfloat16, jnp.float32
        return pl.pallas_call(
            functools.partial(kernel, tiles),
            out_shape=jax.ShapeDtypeStruct(video.shape, bf16),
            in_specs=[any_spec] * 3 + [vmem_spec] * 5,
            out_specs=any_spec,
            scratch_shapes=[
                pltpu.VMEM((frames + 2, rows + 2, cols, chans), bf16),
                pltpu.VMEM((frames + 2, rows + 2, cols, chans), bf16),
                pltpu.VMEM(((frames + 2) * cols, (rows + 2) * 3 * chans), bf16),
                pltpu.VMEM((3, 9 * chans, chans), bf16),
                pltpu.VMEM((3, 9 * chans, chans), bf16),
                pltpu.VMEM((frames * cols, rows * chans), f32),
                pltpu.VMEM(video.shape, bf16),
                pltpu.VMEM((2, 8, chans), f32),
                pltpu.VMEM((2, count - 1, 8, chans), f32),
                pltpu.SemaphoreType.DMA((4,)),
                pltpu.SemaphoreType.DMA((2, 6)),
                pltpu.SemaphoreType.DMA((2, 6)),
            ],
            compiler_params=pltpu.CompilerParams(
                collective_id=0, has_side_effects=True, vmem_limit_bytes=62 * 1024 * 1024
            ),
        )(
            video,
            conv_first.reshape(3, 9 * chans, chans),
            conv_second.reshape(3, 9 * chans, chans),
            *[v.reshape(1, chans) for v in vectors],
        )

    block = P(("grp", "tm"), "tile", None, None)
    return jax.shard_map(
        step, mesh=mesh, in_specs=(block,) + (P(),) * 7, out_specs=block, check_vma=False
    )
```

```python
import functools

import jax
import jax.numpy as jnp
from jax import lax
from jax.experimental import pallas as pl
from jax.experimental.pallas import tpu as pltpu
from jax.sharding import PartitionSpec as P

G = 32
EPSILON = 1e-06
MESH = pl.DeviceIdType.MESH


def group_sums(x, width):
    lanes = x.shape[-1]
    lane = lax.broadcasted_iota(jnp.int32, x.shape, 1)
    step = 1
    while step < width:
        odd = (lane // step) % 2 == 1
        x = x + jnp.where(odd, pltpu.roll(x, step, 1), pltpu.roll(x, lanes - step, 1))
        step *= 2
    return x


def kernel(
    tiles,
    video,
    conv_first,
    conv_second,
    gain_first,
    shift_first,
    gain_second,
    shift_second,
    bias_second,
    out,
    raw,
    hid,
    taps,
    weight_first,
    weight_second,
    first_out,
    result,
    stat_mine,
    stat_got,
    local_sem,
    send_sem,
    recv_sem,
):
    count = tiles * 2
    tile, tm = lax.axis_index("tile"), lax.axis_index("tm")
    cols, chans = raw.shape[2], raw.shape[3]
    cells = float(count * 4 * cols * (chans // G))
    has_up, has_down = tile > 0, tile < tiles - 1

    load_video = pltpu.make_async_copy(video, raw.at[pl.ds(2, 2), pl.ds(0, 2)], local_sem.at[0])
    load_first = pltpu.make_async_copy(conv_first, weight_first, local_sem.at[1])
    load_second = pltpu.make_async_copy(conv_second, weight_second, local_sem.at[2])
    load_video.start()
    load_first.start()
    load_second.start()

    def peer(step, other_core):
        other = tile + step
        return {
            "tile": jnp.where(other >= tiles, other - tiles, other),
            "tm": 1 - tm if other_core else tm,
        }

    def each_peer(visit):
        visit(0, {"tile": tile, "tm": 1 - tm})
        for core in range(2):
            if tiles <= 8:
                for step in range(1, tiles):
                    visit(2 * step - 1 + core, peer(step, core))
            else:

                @pl.loop(1, tiles)
                def _(step):
                    visit(2 * step - 1 + core, peer(step, core))

    barrier = pltpu.get_barrier_semaphore()

    def greet(slot, device):
        pl.semaphore_signal(barrier, inc=1, device_id=device, device_id_type=MESH)

    each_peer(greet)

    @pl.when(jnp.logical_not(has_up))
    def _():
        raw[:, 2] = jnp.zeros((4, cols, chans), jnp.bfloat16)
        hid[:, 2] = jnp.zeros((4, cols, chans), jnp.bfloat16)

    @pl.when(jnp.logical_not(has_down))
    def _():
        raw[:, 3] = jnp.zeros((4, cols, chans), jnp.bfloat16)
        hid[:, 3] = jnp.zeros((4, cols, chans), jnp.bfloat16)

    load_video.wait()

    def put_stats(phase, sums, squares):
        row = lax.broadcasted_iota(jnp.int32, (8, chans), 0)
        stat_mine[phase] = jnp.where(row == 0, sums, jnp.where(row == 1, squares, 0.0))

    def send_stats(phase):
        def send(slot, device):
            pltpu.make_async_remote_copy(
                src_ref=stat_mine.at[phase],
                dst_ref=stat_got.at[phase, slot],
                send_sem=send_sem.at[phase, 10],
                recv_sem=recv_sem.at[phase, 10],
                device_id=device,
                device_id_type=MESH,
            ).start()

        each_peer(send)

    def get_stats(phase, gain):
        got = stat_got.at[phase]
        pltpu.make_async_copy(got, got, recv_sem.at[phase, 10]).wait()
        total = group_sums(stat_mine[phase] + jnp.sum(stat_got[phase], axis=0), chans // G)
        mean = total[0:1] / cells
        spread = total[1:2] / cells - mean * mean
        return mean, lax.rsqrt(spread + EPSILON) * gain

    def copy_of(buf, phase, which, f):
        src, dst, device = {
            "up": (buf.at[2 + f, 0], buf.at[2 + f, 3], {"tile": tile - 1, "tm": tm}),
            "down": (buf.at[2 + f, 1], buf.at[2 + f, 2], {"tile": tile + 1, "tm": tm}),
            "mate": (
                buf.at[2 + f, pl.ds(0, 2)],
                buf.at[f, pl.ds(0, 2)],
                {"tile": tile, "tm": 1 - tm},
            ),
            "mate_top": (buf.at[2 + f, 2], buf.at[f, 2], {"tile": tile, "tm": 1 - tm}),
            "mate_bottom": (buf.at[2 + f, 3], buf.at[f, 3], {"tile": tile, "tm": 1 - tm}),
        }[which]
        at = ("up", "down", "mate", "mate_top", "mate_bottom").index(which) * 2 + f
        return pltpu.make_async_remote_copy(
            src_ref=src,
            dst_ref=dst,
            send_sem=send_sem.at[phase, at],
            recv_sem=recv_sem.at[phase, at],
            device_id=device,
            device_id_type=MESH,
        )

    def send_edges(buf, phase, f):
        @pl.when(has_up)
        def _():
            copy_of(buf, phase, "up", f).start()

        @pl.when(has_down)
        def _():
            copy_of(buf, phase, "down", f).start()

        @pl.when(tm == 0)
        def _():
            copy_of(buf, phase, "mate", f).start()

    def wait_mate(buf, phase):
        @pl.when(tm == 1)
        def _():
            for f in range(2):
                copy_of(buf, phase, "mate", f).wait_recv()

    def wait_edges(buf, phase, f):
        @pl.when(has_up)
        def _():
            copy_of(buf, phase, "down", f).wait_recv()

        @pl.when(tm == 0)
        def _():
            copy_of(buf, phase, "mate_top", f).start()

        @pl.when(has_down)
        def _():
            copy_of(buf, phase, "up", f).wait_recv()

        @pl.when(tm == 0)
        def _():
            copy_of(buf, phase, "mate_bottom", f).start()

    def wait_mate_edges(buf, phase, f):
        @pl.when(tm == 1)
        def _():
            copy_of(buf, phase, "mate_top", f).wait_recv()
            copy_of(buf, phase, "mate_bottom", f).wait_recv()

    def wait_sends(buf, phase):
        got = stat_got.at[phase]
        pltpu.make_async_copy(got, got, send_sem.at[phase, 10]).wait()
        for f in range(2):

            @pl.when(has_up)
            def _():
                copy_of(buf, phase, "up", f).wait_send()

            @pl.when(has_down)
            def _():
                copy_of(buf, phase, "down", f).wait_send()

            @pl.when(tm == 0)
            def _():
                copy_of(buf, phase, "mate", f).wait_send()
                copy_of(buf, phase, "mate_top", f).wait_send()
                copy_of(buf, phase, "mate_bottom", f).wait_send()

    def normalized(values, mean, scale, shift):
        normed = (values - mean) * scale + shift
        return normed * (0.5 + 0.5 * jnp.tanh(0.5 * normed))

    row = lax.broadcasted_iota(jnp.int32, (cols, chans), 0)

    def put_taps(frame, slot, h):
        before = jnp.where(row == 0, 0.0, pltpu.roll(h, 1, 0))
        after = jnp.where(row == cols - 1, 0.0, pltpu.roll(h, cols - 1, 0))
        rows, base = pl.ds(frame * cols, cols), slot * 3 * chans
        taps[rows, base : base + chans] = before.astype(jnp.bfloat16)
        taps[rows, base + chans : base + 2 * chans] = h.astype(jnp.bfloat16)
        taps[rows, base + 2 * chans : base + 3 * chans] = after.astype(jnp.bfloat16)

    wide = 3 * chans
    none = jnp.zeros((wide, chans), jnp.bfloat16)

    def conv_part(weight, part):
        total = None
        for a in range(3):
            w = weight.at[a]
            if part == 0:
                kernel_a = jnp.concatenate([w[wide : 3 * wide], w[0 : 2 * wide]], axis=1)
            else:
                kernel_a = jnp.concatenate(
                    [
                        jnp.concatenate([w[0:wide], none], axis=0),
                        jnp.concatenate([none, w[2 * wide : 3 * wide]], axis=0),
                    ],
                    axis=1,
                )
            x = taps[a * cols : (a + 2) * cols, part * 2 * wide : (part + 1) * 2 * wide]
            y = jnp.dot(x, kernel_a, preferred_element_type=jnp.float32)
            total = y if total is None else total + y
        return total

    own = [(f, s) for f in (2, 3) for s in (0, 1)]
    past = [(f, s) for f in (0, 1) for s in (0, 1)]

    def source_frame(f):
        return jnp.where(tm == 0, 2, f) if f < 2 else f

    sums = jnp.zeros((1, chans), jnp.float32)
    squares = jnp.zeros((1, chans), jnp.float32)
    for f, s in own:
        values = raw[f, s].astype(jnp.float32)
        sums = sums + jnp.sum(values, axis=0, keepdims=True)
        squares = squares + jnp.sum(values * values, axis=0, keepdims=True)
    put_stats(0, sums, squares)
    pl.semaphore_wait(barrier, count - 1)
    send_stats(0)
    for f in range(2):
        send_edges(raw, 0, f)

    mean, scale = get_stats(0, gain_first[...])
    shift = shift_first[...]

    def first_hidden(f, s):
        h = normalized(raw[source_frame(f), s].astype(jnp.float32), mean, scale, shift)
        if s == 2:
            h = jnp.where(has_up, h, 0.0)
        if s == 3:
            h = jnp.where(has_down, h, 0.0)
        put_taps(f, s, h)

    for f, s in own:
        first_hidden(f, s)
    wait_mate(raw, 0)
    for f, s in past:
        first_hidden(f, s)
    load_first.wait()
    first_out[...] = conv_part(weight_first, 0)
    for f in range(2):
        wait_edges(raw, 0, f)
    for f in range(2):
        for s in (2, 3):
            first_hidden(f + 2, s)
    for f in range(2):
        wait_mate_edges(raw, 0, f)
        for s in (2, 3):
            first_hidden(f, s)
    first = first_out[...] + conv_part(weight_first, 1)
    first_out[...] = first

    sums = jnp.sum(first, axis=0, keepdims=True)
    squares = jnp.sum(first * first, axis=0, keepdims=True)
    put_stats(1, sums[:, :chans] + sums[:, chans:], squares[:, :chans] + squares[:, chans:])
    send_stats(1)
    mean, scale = get_stats(1, gain_second[...])
    shift = shift_second[...]
    for f, s in own:
        h = normalized(
            first_out[(f - 2) * cols : (f - 1) * cols, s * chans : (s + 1) * chans],
            mean,
            scale,
            shift,
        )
        hid[f, s] = h.astype(jnp.bfloat16)
        if s == 1:
            send_edges(hid, 1, f - 2)

    def second_hidden(f, s):
        put_taps(f, s, hid[source_frame(f), s].astype(jnp.float32))

    for f, s in own:
        second_hidden(f, s)
    wait_mate(hid, 1)
    for f, s in past:
        second_hidden(f, s)
    load_second.wait()
    first_out[...] = conv_part(weight_second, 0)
    for f in range(2):
        wait_edges(hid, 1, f)
    for f in range(2):
        for s in (2, 3):
            second_hidden(f + 2, s)
    for f in range(2):
        wait_mate_edges(hid, 1, f)
        for s in (2, 3):
            second_hidden(f, s)
    branch = first_out[...] + conv_part(weight_second, 1)
    bias = bias_second[...]
    for f, s in own:
        value = branch[(f - 2) * cols : (f - 1) * cols, s * chans : (s + 1) * chans]
        result[f - 2, s] = (raw[f, s].astype(jnp.float32) + value + bias).astype(jnp.bfloat16)
    store = pltpu.make_async_copy(result, out, local_sem.at[3])
    store.start()
    wait_sends(raw, 0)
    wait_sends(hid, 1)
    store.wait()


def solution(mesh):
    tiles = mesh.shape["tile"]
    count = tiles * mesh.shape["tm"]

    def step(video, conv_first, conv_second, *vectors):
        frames, rows, cols, chans = video.shape
        any_spec = pl.BlockSpec(memory_space=pl.ANY)
        vmem_spec = pl.BlockSpec(memory_space=pltpu.VMEM)
        bf16, f32 = jnp.bfloat16, jnp.float32
        return pl.pallas_call(
            functools.partial(kernel, tiles),
            out_shape=jax.ShapeDtypeStruct(video.shape, bf16),
            in_specs=[any_spec] * 3 + [vmem_spec] * 5,
            out_specs=any_spec,
            scratch_shapes=[
                pltpu.VMEM((frames + 2, rows + 2, cols, chans), bf16),
                pltpu.VMEM((frames + 2, rows + 2, cols, chans), bf16),
                pltpu.VMEM(((frames + 2) * cols, (rows + 2) * 3 * chans), bf16),
                pltpu.VMEM((3, 9 * chans, chans), bf16),
                pltpu.VMEM((3, 9 * chans, chans), bf16),
                pltpu.VMEM((frames * cols, rows * chans), f32),
                pltpu.VMEM(video.shape, bf16),
                pltpu.VMEM((2, 8, chans), f32),
                pltpu.VMEM((2, count - 1, 8, chans), f32),
                pltpu.SemaphoreType.DMA((4,)),
                pltpu.SemaphoreType.DMA((2, 11)),
                pltpu.SemaphoreType.DMA((2, 11)),
            ],
            compiler_params=pltpu.CompilerParams(
                collective_id=0, has_side_effects=True, vmem_limit_bytes=62 * 1024 * 1024
            ),
        )(
            video,
            conv_first.reshape(3, 9 * chans, chans),
            conv_second.reshape(3, 9 * chans, chans),
            *[v.reshape(1, chans) for v in vectors],
        )

    block = P(("grp", "tm"), "tile", None, None)
    return jax.shard_map(
        step, mesh=mesh, in_specs=(block,) + (P(),) * 7, out_specs=block, check_vma=False
    )
```

```python
import functools

import jax
import jax.numpy as jnp
from jax import lax
from jax.experimental import pallas as pl
from jax.experimental.pallas import tpu as pltpu
from jax.sharding import PartitionSpec as P

G = 32
EPSILON = 1e-06
MESH = pl.DeviceIdType.MESH


def group_sums(x, width):
    lanes = x.shape[-1]
    lane = lax.broadcasted_iota(jnp.int32, x.shape, 1)
    step = 1
    while step < width:
        odd = (lane // step) % 2 == 1
        x = x + jnp.where(odd, pltpu.roll(x, step, 1), pltpu.roll(x, lanes - step, 1))
        step *= 2
    return x


def kernel(
    tiles,
    video,
    conv_first,
    conv_second,
    gain_first,
    shift_first,
    gain_second,
    shift_second,
    bias_second,
    out,
    raw,
    hid,
    taps,
    weight_first,
    weight_second,
    first_out,
    result,
    stat_mine,
    stat_got,
    local_sem,
    send_sem,
    recv_sem,
):
    count = tiles * 2
    tile, tm = lax.axis_index("tile"), lax.axis_index("tm")
    cols, chans = raw.shape[2], raw.shape[3]
    cells = float(count * 4 * cols * (chans // G))
    has_up, has_down = tile > 0, tile < tiles - 1

    load_video = pltpu.make_async_copy(video, raw.at[pl.ds(2, 2), pl.ds(0, 2)], local_sem.at[0])
    load_first = pltpu.make_async_copy(conv_first, weight_first, local_sem.at[1])
    load_second = pltpu.make_async_copy(conv_second, weight_second, local_sem.at[2])
    load_video.start()
    load_first.start()
    load_second.start()

    def peer(step, other_core):
        other = tile + step
        return {
            "tile": jnp.where(other >= tiles, other - tiles, other),
            "tm": 1 - tm if other_core else tm,
        }

    def each_peer(visit):
        visit(0, {"tile": tile, "tm": 1 - tm})
        for core in range(2):
            if tiles <= 8:
                for step in range(1, tiles):
                    visit(2 * step - 1 + core, peer(step, core))
            else:

                @pl.loop(1, tiles)
                def _(step):
                    visit(2 * step - 1 + core, peer(step, core))

    barrier = pltpu.get_barrier_semaphore()

    def greet(slot, device):
        pl.semaphore_signal(barrier, inc=1, device_id=device, device_id_type=MESH)

    each_peer(greet)

    @pl.when(jnp.logical_not(has_up))
    def _():
        raw[:, 2] = jnp.zeros((4, cols, chans), jnp.bfloat16)
        hid[:, 2] = jnp.zeros((4, cols, chans), jnp.bfloat16)

    @pl.when(jnp.logical_not(has_down))
    def _():
        raw[:, 3] = jnp.zeros((4, cols, chans), jnp.bfloat16)
        hid[:, 3] = jnp.zeros((4, cols, chans), jnp.bfloat16)

    load_video.wait()

    def put_stats(phase, sums, squares):
        row = lax.broadcasted_iota(jnp.int32, (8, chans), 0)
        stat_mine[phase] = jnp.where(row == 0, sums, jnp.where(row == 1, squares, 0.0))

    def send_stats(phase):
        def send(slot, device):
            pltpu.make_async_remote_copy(
                src_ref=stat_mine.at[phase],
                dst_ref=stat_got.at[phase, slot],
                send_sem=send_sem.at[phase, 10],
                recv_sem=recv_sem.at[phase, 10],
                device_id=device,
                device_id_type=MESH,
            ).start()

        each_peer(send)

    def get_stats(phase, gain):
        got = stat_got.at[phase]
        pltpu.make_async_copy(got, got, recv_sem.at[phase, 10]).wait()
        total = group_sums(stat_mine[phase] + jnp.sum(stat_got[phase], axis=0), chans // G)
        mean = total[0:1] / cells
        spread = total[1:2] / cells - mean * mean
        return mean, lax.rsqrt(spread + EPSILON) * gain

    def copy_of(buf, phase, which, f):
        src, dst, device = {
            "up": (buf.at[2 + f, 0], buf.at[2 + f, 3], {"tile": tile - 1, "tm": tm}),
            "down": (buf.at[2 + f, 1], buf.at[2 + f, 2], {"tile": tile + 1, "tm": tm}),
            "mate": (
                buf.at[2 + f, pl.ds(0, 2)],
                buf.at[f, pl.ds(0, 2)],
                {"tile": tile, "tm": 1 - tm},
            ),
            "mate_top": (buf.at[2 + f, 2], buf.at[f, 2], {"tile": tile, "tm": 1 - tm}),
            "mate_bottom": (buf.at[2 + f, 3], buf.at[f, 3], {"tile": tile, "tm": 1 - tm}),
        }[which]
        at = ("up", "down", "mate", "mate_top", "mate_bottom").index(which) * 2 + f
        return pltpu.make_async_remote_copy(
            src_ref=src,
            dst_ref=dst,
            send_sem=send_sem.at[phase, at],
            recv_sem=recv_sem.at[phase, at],
            device_id=device,
            device_id_type=MESH,
        )

    def send_edges(buf, phase, f):
        @pl.when(has_up)
        def _():
            copy_of(buf, phase, "up", f).start()

        @pl.when(has_down)
        def _():
            copy_of(buf, phase, "down", f).start()

        @pl.when(tm == 0)
        def _():
            copy_of(buf, phase, "mate", f).start()

    def wait_mate(buf, phase):
        @pl.when(tm == 1)
        def _():
            for f in range(2):
                copy_of(buf, phase, "mate", f).wait_recv()

    def wait_edges(buf, phase, f):
        @pl.when(has_up)
        def _():
            copy_of(buf, phase, "down", f).wait_recv()

        @pl.when(tm == 0)
        def _():
            copy_of(buf, phase, "mate_top", f).start()

        @pl.when(has_down)
        def _():
            copy_of(buf, phase, "up", f).wait_recv()

        @pl.when(tm == 0)
        def _():
            copy_of(buf, phase, "mate_bottom", f).start()

    def wait_mate_edges(buf, phase, f):
        @pl.when(tm == 1)
        def _():
            copy_of(buf, phase, "mate_top", f).wait_recv()
            copy_of(buf, phase, "mate_bottom", f).wait_recv()

    def wait_sends(buf, phase):
        got = stat_got.at[phase]
        pltpu.make_async_copy(got, got, send_sem.at[phase, 10]).wait()
        for f in range(2):

            @pl.when(has_up)
            def _():
                copy_of(buf, phase, "up", f).wait_send()

            @pl.when(has_down)
            def _():
                copy_of(buf, phase, "down", f).wait_send()

            @pl.when(tm == 0)
            def _():
                copy_of(buf, phase, "mate", f).wait_send()
                copy_of(buf, phase, "mate_top", f).wait_send()
                copy_of(buf, phase, "mate_bottom", f).wait_send()

    def normalized(values, mean, scale, shift):
        normed = (values - mean) * scale + shift
        return normed * (0.5 + 0.5 * jnp.tanh(0.5 * normed))

    row = lax.broadcasted_iota(jnp.int32, (cols, chans), 0)

    def put_taps(frame, slot, h):
        before = jnp.where(row == 0, 0.0, pltpu.roll(h, 1, 0))
        after = jnp.where(row == cols - 1, 0.0, pltpu.roll(h, cols - 1, 0))
        rows, base = pl.ds(frame * cols, cols), slot * 3 * chans
        taps[rows, base : base + chans] = before.astype(jnp.bfloat16)
        taps[rows, base + chans : base + 2 * chans] = h.astype(jnp.bfloat16)
        taps[rows, base + 2 * chans : base + 3 * chans] = after.astype(jnp.bfloat16)

    wide = 3 * chans
    none = jnp.zeros((wide, chans), jnp.bfloat16)

    def conv_part(weight, part, times):
        total = None
        for a in times:
            w = weight.at[a]
            if part == 0:
                kernel_a = jnp.concatenate([w[wide : 3 * wide], w[0 : 2 * wide]], axis=1)
            else:
                kernel_a = jnp.concatenate(
                    [
                        jnp.concatenate([w[0:wide], none], axis=0),
                        jnp.concatenate([none, w[2 * wide : 3 * wide]], axis=0),
                    ],
                    axis=1,
                )
            x = taps[a * cols : (a + 2) * cols, part * 2 * wide : (part + 1) * 2 * wide]
            y = jnp.dot(x, kernel_a, preferred_element_type=jnp.float32)
            total = y if total is None else total + y
        return total

    own = [(f, s) for f in (2, 3) for s in (0, 1)]
    past = [(f, s) for f in (0, 1) for s in (0, 1)]

    def source_frame(f):
        return jnp.where(tm == 0, 2, f) if f < 2 else f

    sums = jnp.zeros((1, chans), jnp.float32)
    squares = jnp.zeros((1, chans), jnp.float32)
    for f, s in own:
        values = raw[f, s].astype(jnp.float32)
        sums = sums + jnp.sum(values, axis=0, keepdims=True)
        squares = squares + jnp.sum(values * values, axis=0, keepdims=True)
    put_stats(0, sums, squares)
    pl.semaphore_wait(barrier, count - 1)
    send_stats(0)
    for f in range(2):
        send_edges(raw, 0, f)

    mean, scale = get_stats(0, gain_first[...])
    shift = shift_first[...]

    def first_hidden(f, s):
        h = normalized(raw[source_frame(f), s].astype(jnp.float32), mean, scale, shift)
        if s == 2:
            h = jnp.where(has_up, h, 0.0)
        if s == 3:
            h = jnp.where(has_down, h, 0.0)
        put_taps(f, s, h)

    for f, s in own:
        first_hidden(f, s)
    load_first.wait()
    first_out[...] = conv_part(weight_first, 0, (2,))
    wait_mate(raw, 0)
    for f, s in past:
        first_hidden(f, s)
    first_out[...] = first_out[...] + conv_part(weight_first, 0, (0, 1))
    for f in range(2):
        wait_edges(raw, 0, f)
    for f in range(2):
        for s in (2, 3):
            first_hidden(f + 2, s)
    first_out[...] = first_out[...] + conv_part(weight_first, 1, (2,))
    for f in range(2):
        wait_mate_edges(raw, 0, f)
        for s in (2, 3):
            first_hidden(f, s)
    first = first_out[...] + conv_part(weight_first, 1, (0, 1))
    first_out[...] = first

    sums = jnp.sum(first, axis=0, keepdims=True)
    squares = jnp.sum(first * first, axis=0, keepdims=True)
    put_stats(1, sums[:, :chans] + sums[:, chans:], squares[:, :chans] + squares[:, chans:])
    send_stats(1)
    mean, scale = get_stats(1, gain_second[...])
    shift = shift_second[...]
    for f, s in own:
        h = normalized(
            first_out[(f - 2) * cols : (f - 1) * cols, s * chans : (s + 1) * chans],
            mean,
            scale,
            shift,
        )
        hid[f, s] = h.astype(jnp.bfloat16)
        if s == 1:
            send_edges(hid, 1, f - 2)

    def second_hidden(f, s):
        put_taps(f, s, hid[source_frame(f), s].astype(jnp.float32))

    for f, s in own:
        second_hidden(f, s)
    load_second.wait()
    first_out[...] = conv_part(weight_second, 0, (2,))
    wait_mate(hid, 1)
    for f, s in past:
        second_hidden(f, s)
    first_out[...] = first_out[...] + conv_part(weight_second, 0, (0, 1))
    for f in range(2):
        wait_edges(hid, 1, f)
    for f in range(2):
        for s in (2, 3):
            second_hidden(f + 2, s)
    first_out[...] = first_out[...] + conv_part(weight_second, 1, (2,))
    for f in range(2):
        wait_mate_edges(hid, 1, f)
        for s in (2, 3):
            second_hidden(f, s)
    branch = first_out[...] + conv_part(weight_second, 1, (0, 1))
    bias = bias_second[...]
    for f, s in own:
        value = branch[(f - 2) * cols : (f - 1) * cols, s * chans : (s + 1) * chans]
        result[f - 2, s] = (raw[f, s].astype(jnp.float32) + value + bias).astype(jnp.bfloat16)
    store = pltpu.make_async_copy(result, out, local_sem.at[3])
    store.start()
    wait_sends(raw, 0)
    wait_sends(hid, 1)
    store.wait()


def solution(mesh):
    tiles = mesh.shape["tile"]
    count = tiles * mesh.shape["tm"]

    def step(video, conv_first, conv_second, *vectors):
        frames, rows, cols, chans = video.shape
        any_spec = pl.BlockSpec(memory_space=pl.ANY)
        vmem_spec = pl.BlockSpec(memory_space=pltpu.VMEM)
        bf16, f32 = jnp.bfloat16, jnp.float32
        return pl.pallas_call(
            functools.partial(kernel, tiles),
            out_shape=jax.ShapeDtypeStruct(video.shape, bf16),
            in_specs=[any_spec] * 3 + [vmem_spec] * 5,
            out_specs=any_spec,
            scratch_shapes=[
                pltpu.VMEM((frames + 2, rows + 2, cols, chans), bf16),
                pltpu.VMEM((frames + 2, rows + 2, cols, chans), bf16),
                pltpu.VMEM(((frames + 2) * cols, (rows + 2) * 3 * chans), bf16),
                pltpu.VMEM((3, 9 * chans, chans), bf16),
                pltpu.VMEM((3, 9 * chans, chans), bf16),
                pltpu.VMEM((frames * cols, rows * chans), f32),
                pltpu.VMEM(video.shape, bf16),
                pltpu.VMEM((2, 8, chans), f32),
                pltpu.VMEM((2, count - 1, 8, chans), f32),
                pltpu.SemaphoreType.DMA((4,)),
                pltpu.SemaphoreType.DMA((2, 11)),
                pltpu.SemaphoreType.DMA((2, 11)),
            ],
            compiler_params=pltpu.CompilerParams(
                collective_id=0, has_side_effects=True, vmem_limit_bytes=62 * 1024 * 1024
            ),
        )(
            video,
            conv_first.reshape(3, 9 * chans, chans),
            conv_second.reshape(3, 9 * chans, chans),
            *[v.reshape(1, chans) for v in vectors],
        )

    block = P(("grp", "tm"), "tile", None, None)
    return jax.shard_map(
        step, mesh=mesh, in_specs=(block,) + (P(),) * 7, out_specs=block, check_vma=False
    )
```

```python
import functools

import jax
import jax.numpy as jnp
from jax import lax
from jax.experimental import pallas as pl
from jax.experimental.pallas import tpu as pltpu
from jax.sharding import PartitionSpec as P

G = 32
EPSILON = 1e-06
MESH = pl.DeviceIdType.MESH


def group_sums(x, width):
    lanes = x.shape[-1]
    lane = lax.broadcasted_iota(jnp.int32, x.shape, 1)
    step = 1
    while step < width:
        odd = (lane // step) % 2 == 1
        x = x + jnp.where(odd, pltpu.roll(x, step, 1), pltpu.roll(x, lanes - step, 1))
        step *= 2
    return x


def kernel(
    tiles,
    video,
    conv_first,
    conv_second,
    gain_first,
    shift_first,
    gain_second,
    shift_second,
    bias_second,
    out,
    raw,
    hid,
    taps,
    weight_first,
    weight_second,
    first_out,
    result,
    stat_mine,
    stat_got,
    local_sem,
    send_sem,
    recv_sem,
):
    count = tiles * 2
    tile, tm = lax.axis_index("tile"), lax.axis_index("tm")
    cols, chans = raw.shape[2], raw.shape[3]
    cells = float(count * 4 * cols * (chans // G))
    has_up, has_down = tile > 0, tile < tiles - 1

    load_video = pltpu.make_async_copy(video, raw.at[pl.ds(2, 2), pl.ds(0, 2)], local_sem.at[0])
    load_first = pltpu.make_async_copy(conv_first, weight_first, local_sem.at[1])
    load_second = pltpu.make_async_copy(conv_second, weight_second, local_sem.at[2])
    load_video.start()
    load_first.start()
    load_second.start()

    def peer(step, other_core):
        other = tile + step
        return {
            "tile": jnp.where(other >= tiles, other - tiles, other),
            "tm": 1 - tm if other_core else tm,
        }

    def each_peer(visit):
        visit(0, {"tile": tile, "tm": 1 - tm})
        for core in range(2):
            if tiles <= 8:
                for step in range(1, tiles):
                    visit(2 * step - 1 + core, peer(step, core))
            else:

                @pl.loop(1, tiles)
                def _(step):
                    visit(2 * step - 1 + core, peer(step, core))

    barrier = pltpu.get_barrier_semaphore()

    def greet(slot, device):
        pl.semaphore_signal(barrier, inc=1, device_id=device, device_id_type=MESH)

    each_peer(greet)

    @pl.when(jnp.logical_not(has_up))
    def _():
        raw[:, 2] = jnp.zeros((4, cols, chans), jnp.bfloat16)
        hid[:, 2] = jnp.zeros((4, cols, chans), jnp.bfloat16)

    @pl.when(jnp.logical_not(has_down))
    def _():
        raw[:, 3] = jnp.zeros((4, cols, chans), jnp.bfloat16)
        hid[:, 3] = jnp.zeros((4, cols, chans), jnp.bfloat16)

    load_video.wait()

    def put_stats(phase, sums, squares):
        row = lax.broadcasted_iota(jnp.int32, (8, chans), 0)
        stat_mine[phase] = jnp.where(row == 0, sums, jnp.where(row == 1, squares, 0.0))

    def send_stats(phase):
        def send(slot, device):
            pltpu.make_async_remote_copy(
                src_ref=stat_mine.at[phase],
                dst_ref=stat_got.at[phase, slot],
                send_sem=send_sem.at[phase, 10],
                recv_sem=recv_sem.at[phase, 10],
                device_id=device,
                device_id_type=MESH,
            ).start()

        each_peer(send)

    def get_stats(phase, gain):
        got = stat_got.at[phase]
        pltpu.make_async_copy(got, got, recv_sem.at[phase, 10]).wait()
        total = group_sums(stat_mine[phase] + jnp.sum(stat_got[phase], axis=0), chans // G)
        mean = total[0:1] / cells
        spread = total[1:2] / cells - mean * mean
        return mean, lax.rsqrt(spread + EPSILON) * gain

    def copy_of(buf, phase, which, f):
        src, dst, device = {
            "up": (buf.at[2 + f, 0], buf.at[2 + f, 3], {"tile": tile - 1, "tm": tm}),
            "down": (buf.at[2 + f, 1], buf.at[2 + f, 2], {"tile": tile + 1, "tm": tm}),
            "mate": (
                buf.at[2 + f, pl.ds(0, 2)],
                buf.at[f, pl.ds(0, 2)],
                {"tile": tile, "tm": 1 - tm},
            ),
            "mate_top": (buf.at[2 + f, 2], buf.at[f, 2], {"tile": tile, "tm": 1 - tm}),
            "mate_bottom": (buf.at[2 + f, 3], buf.at[f, 3], {"tile": tile, "tm": 1 - tm}),
        }[which]
        at = ("up", "down", "mate", "mate_top", "mate_bottom").index(which) * 2 + f
        return pltpu.make_async_remote_copy(
            src_ref=src,
            dst_ref=dst,
            send_sem=send_sem.at[phase, at],
            recv_sem=recv_sem.at[phase, at],
            device_id=device,
            device_id_type=MESH,
        )

    def send_edges(buf, phase, f):
        @pl.when(has_up)
        def _():
            copy_of(buf, phase, "up", f).start()

        @pl.when(has_down)
        def _():
            copy_of(buf, phase, "down", f).start()

        @pl.when(tm == 0)
        def _():
            copy_of(buf, phase, "mate", f).start()

    def wait_mate(buf, phase):
        @pl.when(tm == 1)
        def _():
            for f in range(2):
                copy_of(buf, phase, "mate", f).wait_recv()

    def wait_edges(buf, phase, f):
        @pl.when(has_up)
        def _():
            copy_of(buf, phase, "down", f).wait_recv()

        @pl.when(tm == 0)
        def _():
            copy_of(buf, phase, "mate_top", f).start()

        @pl.when(has_down)
        def _():
            copy_of(buf, phase, "up", f).wait_recv()

        @pl.when(tm == 0)
        def _():
            copy_of(buf, phase, "mate_bottom", f).start()

    def wait_mate_edges(buf, phase, f):
        @pl.when(tm == 1)
        def _():
            copy_of(buf, phase, "mate_top", f).wait_recv()
            copy_of(buf, phase, "mate_bottom", f).wait_recv()

    def wait_sends(buf, phase):
        got = stat_got.at[phase]
        pltpu.make_async_copy(got, got, send_sem.at[phase, 10]).wait()
        for f in range(2):

            @pl.when(has_up)
            def _():
                copy_of(buf, phase, "up", f).wait_send()

            @pl.when(has_down)
            def _():
                copy_of(buf, phase, "down", f).wait_send()

            @pl.when(tm == 0)
            def _():
                copy_of(buf, phase, "mate", f).wait_send()
                copy_of(buf, phase, "mate_top", f).wait_send()
                copy_of(buf, phase, "mate_bottom", f).wait_send()

    def normalized(values, mean, scale, shift):
        normed = (values - mean) * scale + shift
        return normed * (0.5 + 0.5 * jnp.tanh(0.5 * normed))

    row = lax.broadcasted_iota(jnp.int32, (cols, chans), 0)

    def put_taps(frame, slot, h):
        before = jnp.where(row == 0, 0.0, pltpu.roll(h, 1, 0))
        after = jnp.where(row == cols - 1, 0.0, pltpu.roll(h, cols - 1, 0))
        rows, base = pl.ds(frame * cols, cols), slot * 3 * chans
        taps[rows, base : base + chans] = before.astype(jnp.bfloat16)
        taps[rows, base + chans : base + 2 * chans] = h.astype(jnp.bfloat16)
        taps[rows, base + 2 * chans : base + 3 * chans] = after.astype(jnp.bfloat16)

    wide = 3 * chans
    none = jnp.zeros((wide, chans), jnp.bfloat16)

    def conv_part(weight, part, times):
        total = None
        for a in times:
            w = weight.at[a]
            if part == 0:
                kernel_a = jnp.concatenate([w[wide : 3 * wide], w[0 : 2 * wide]], axis=1)
            else:
                kernel_a = jnp.concatenate(
                    [
                        jnp.concatenate([w[0:wide], none], axis=0),
                        jnp.concatenate([none, w[2 * wide : 3 * wide]], axis=0),
                    ],
                    axis=1,
                )
            x = taps[a * cols : (a + 2) * cols, part * 2 * wide : (part + 1) * 2 * wide]
            y = jnp.dot(x, kernel_a, preferred_element_type=jnp.float32)
            total = y if total is None else total + y
        return total

    own = [(f, s) for f in (2, 3) for s in (0, 1)]
    past = [(f, s) for f in (0, 1) for s in (0, 1)]

    def source_frame(f):
        return jnp.where(tm == 0, 2, f) if f < 2 else f

    sums = jnp.zeros((1, chans), jnp.float32)
    squares = jnp.zeros((1, chans), jnp.float32)
    for f, s in own:
        values = raw[f, s].astype(jnp.float32)
        sums = sums + jnp.sum(values, axis=0, keepdims=True)
        squares = squares + jnp.sum(values * values, axis=0, keepdims=True)
    put_stats(0, sums, squares)
    pl.semaphore_wait(barrier, count - 1)
    send_stats(0)
    for f in range(2):
        send_edges(raw, 0, f)

    mean, scale = get_stats(0, gain_first[...])
    shift = shift_first[...]

    def first_hidden(f, s):
        h = normalized(raw[source_frame(f), s].astype(jnp.float32), mean, scale, shift)
        if s == 2:
            h = jnp.where(has_up, h, 0.0)
        if s == 3:
            h = jnp.where(has_down, h, 0.0)
        put_taps(f, s, h)

    for f, s in own:
        first_hidden(f, s)
    load_first.wait()
    first_out[...] = conv_part(weight_first, 0, (2,))
    wait_mate(raw, 0)
    for f, s in past:
        first_hidden(f, s)
    first_out[...] = first_out[...] + conv_part(weight_first, 0, (0, 1))
    for f in range(2):
        wait_edges(raw, 0, f)
        for s in (2, 3):
            first_hidden(f + 2, s)
    first_out[...] = first_out[...] + conv_part(weight_first, 1, (2,))
    for f in range(2):
        wait_mate_edges(raw, 0, f)
        for s in (2, 3):
            first_hidden(f, s)
    first = first_out[...] + conv_part(weight_first, 1, (0, 1))
    first_out[...] = first

    sums = jnp.sum(first, axis=0, keepdims=True)
    squares = jnp.sum(first * first, axis=0, keepdims=True)
    put_stats(1, sums[:, :chans] + sums[:, chans:], squares[:, :chans] + squares[:, chans:])
    send_stats(1)
    mean, scale = get_stats(1, gain_second[...])
    shift = shift_second[...]
    for f, s in own:
        h = normalized(
            first_out[(f - 2) * cols : (f - 1) * cols, s * chans : (s + 1) * chans],
            mean,
            scale,
            shift,
        )
        hid[f, s] = h.astype(jnp.bfloat16)
        if s == 1:
            send_edges(hid, 1, f - 2)

    def second_hidden(f, s):
        put_taps(f, s, hid[source_frame(f), s].astype(jnp.float32))

    for f, s in own:
        second_hidden(f, s)
    load_second.wait()
    first_out[...] = conv_part(weight_second, 0, (2,))
    wait_mate(hid, 1)
    for f, s in past:
        second_hidden(f, s)
    first_out[...] = first_out[...] + conv_part(weight_second, 0, (0, 1))
    for f in range(2):
        wait_edges(hid, 1, f)
        for s in (2, 3):
            second_hidden(f + 2, s)
    first_out[...] = first_out[...] + conv_part(weight_second, 1, (2,))
    for f in range(2):
        wait_mate_edges(hid, 1, f)
        for s in (2, 3):
            second_hidden(f, s)
    branch = first_out[...] + conv_part(weight_second, 1, (0, 1))
    bias = bias_second[...]
    for f, s in own:
        value = branch[(f - 2) * cols : (f - 1) * cols, s * chans : (s + 1) * chans]
        result[f - 2, s] = (raw[f, s].astype(jnp.float32) + value + bias).astype(jnp.bfloat16)
    store = pltpu.make_async_copy(result, out, local_sem.at[3])
    store.start()
    wait_sends(raw, 0)
    wait_sends(hid, 1)
    store.wait()


def solution(mesh):
    tiles = mesh.shape["tile"]
    count = tiles * mesh.shape["tm"]

    def step(video, conv_first, conv_second, *vectors):
        frames, rows, cols, chans = video.shape
        any_spec = pl.BlockSpec(memory_space=pl.ANY)
        vmem_spec = pl.BlockSpec(memory_space=pltpu.VMEM)
        bf16, f32 = jnp.bfloat16, jnp.float32
        return pl.pallas_call(
            functools.partial(kernel, tiles),
            out_shape=jax.ShapeDtypeStruct(video.shape, bf16),
            in_specs=[any_spec] * 3 + [vmem_spec] * 5,
            out_specs=any_spec,
            scratch_shapes=[
                pltpu.VMEM((frames + 2, rows + 2, cols, chans), bf16),
                pltpu.VMEM((frames + 2, rows + 2, cols, chans), bf16),
                pltpu.VMEM(((frames + 2) * cols, (rows + 2) * 3 * chans), bf16),
                pltpu.VMEM((3, 9 * chans, chans), bf16),
                pltpu.VMEM((3, 9 * chans, chans), bf16),
                pltpu.VMEM((frames * cols, rows * chans), f32),
                pltpu.VMEM(video.shape, bf16),
                pltpu.VMEM((2, 8, chans), f32),
                pltpu.VMEM((2, count - 1, 8, chans), f32),
                pltpu.SemaphoreType.DMA((4,)),
                pltpu.SemaphoreType.DMA((2, 11)),
                pltpu.SemaphoreType.DMA((2, 11)),
            ],
            compiler_params=pltpu.CompilerParams(
                collective_id=0, has_side_effects=True, vmem_limit_bytes=62 * 1024 * 1024
            ),
        )(
            video,
            conv_first.reshape(3, 9 * chans, chans),
            conv_second.reshape(3, 9 * chans, chans),
            *[v.reshape(1, chans) for v in vectors],
        )

    block = P(("grp", "tm"), "tile", None, None)
    return jax.shard_map(
        step, mesh=mesh, in_specs=(block,) + (P(),) * 7, out_specs=block, check_vma=False
    )
```

```python
import functools

import jax
import jax.numpy as jnp
from jax import lax
from jax.experimental import pallas as pl
from jax.experimental.pallas import tpu as pltpu
from jax.sharding import PartitionSpec as P

G = 32
EPSILON = 1e-06
MESH = pl.DeviceIdType.MESH


def group_sums(x, width):
    lanes = x.shape[-1]
    lane = lax.broadcasted_iota(jnp.int32, x.shape, 1)
    step = 1
    while step < width:
        odd = (lane // step) % 2 == 1
        x = x + jnp.where(odd, pltpu.roll(x, step, 1), pltpu.roll(x, lanes - step, 1))
        step *= 2
    return x


def kernel(
    tiles,
    video,
    conv_first,
    conv_second,
    gain_first,
    shift_first,
    gain_second,
    shift_second,
    bias_second,
    out,
    raw,
    hid,
    taps,
    weight_first,
    weight_second,
    first_out,
    result,
    stat_mine,
    stat_got,
    local_sem,
    send_sem,
    recv_sem,
):
    count = tiles * 2
    tile, tm = lax.axis_index("tile"), lax.axis_index("tm")
    cols, chans = raw.shape[2], raw.shape[3]
    cells = float(count * 4 * cols * (chans // G))
    has_up, has_down = tile > 0, tile < tiles - 1

    load_video = pltpu.make_async_copy(video, raw.at[pl.ds(2, 2), pl.ds(0, 2)], local_sem.at[0])
    load_first = pltpu.make_async_copy(conv_first, weight_first, local_sem.at[1])
    load_second = pltpu.make_async_copy(conv_second, weight_second, local_sem.at[2])
    load_video.start()

    def peer(step, other_core):
        other = tile + step
        return {
            "tile": jnp.where(other >= tiles, other - tiles, other),
            "tm": 1 - tm if other_core else tm,
        }

    def each_peer(visit):
        visit(0, {"tile": tile, "tm": 1 - tm})
        for core in range(2):
            if tiles <= 8:
                for step in range(1, tiles):
                    visit(2 * step - 1 + core, peer(step, core))
            else:

                @pl.loop(1, tiles)
                def _(step):
                    visit(2 * step - 1 + core, peer(step, core))

    barrier = pltpu.get_barrier_semaphore()

    def greet(slot, device):
        pl.semaphore_signal(barrier, inc=1, device_id=device, device_id_type=MESH)

    each_peer(greet)
    load_first.start()
    load_second.start()

    @pl.when(jnp.logical_not(has_up))
    def _():
        raw[:, 2] = jnp.zeros((4, cols, chans), jnp.bfloat16)
        hid[:, 2] = jnp.zeros((4, cols, chans), jnp.bfloat16)

    @pl.when(jnp.logical_not(has_down))
    def _():
        raw[:, 3] = jnp.zeros((4, cols, chans), jnp.bfloat16)
        hid[:, 3] = jnp.zeros((4, cols, chans), jnp.bfloat16)

    load_video.wait()

    def put_stats(phase, sums, squares):
        row = lax.broadcasted_iota(jnp.int32, (8, chans), 0)
        stat_mine[phase] = jnp.where(row == 0, sums, jnp.where(row == 1, squares, 0.0))

    def send_stats(phase):
        def send(slot, device):
            pltpu.make_async_remote_copy(
                src_ref=stat_mine.at[phase],
                dst_ref=stat_got.at[phase, slot],
                send_sem=send_sem.at[phase, 10],
                recv_sem=recv_sem.at[phase, 10],
                device_id=device,
                device_id_type=MESH,
            ).start()

        each_peer(send)

    def get_stats(phase, gain):
        got = stat_got.at[phase]
        pltpu.make_async_copy(got, got, recv_sem.at[phase, 10]).wait()
        total = group_sums(stat_mine[phase] + jnp.sum(stat_got[phase], axis=0), chans // G)
        mean = total[0:1] / cells
        spread = total[1:2] / cells - mean * mean
        return mean, lax.rsqrt(spread + EPSILON) * gain

    def copy_of(buf, phase, which, f):
        src, dst, device = {
            "up": (buf.at[2 + f, 0], buf.at[2 + f, 3], {"tile": tile - 1, "tm": tm}),
            "down": (buf.at[2 + f, 1], buf.at[2 + f, 2], {"tile": tile + 1, "tm": tm}),
            "mate": (
                buf.at[2 + f, pl.ds(0, 2)],
                buf.at[f, pl.ds(0, 2)],
                {"tile": tile, "tm": 1 - tm},
            ),
            "mate_top": (buf.at[2 + f, 2], buf.at[f, 2], {"tile": tile, "tm": 1 - tm}),
            "mate_bottom": (buf.at[2 + f, 3], buf.at[f, 3], {"tile": tile, "tm": 1 - tm}),
        }[which]
        at = ("up", "down", "mate", "mate_top", "mate_bottom").index(which) * 2 + f
        return pltpu.make_async_remote_copy(
            src_ref=src,
            dst_ref=dst,
            send_sem=send_sem.at[phase, at],
            recv_sem=recv_sem.at[phase, at],
            device_id=device,
            device_id_type=MESH,
        )

    def send_edges(buf, phase, f):
        @pl.when(has_up)
        def _():
            copy_of(buf, phase, "up", f).start()

        @pl.when(has_down)
        def _():
            copy_of(buf, phase, "down", f).start()

        @pl.when(tm == 0)
        def _():
            copy_of(buf, phase, "mate", f).start()

    def wait_mate(buf, phase):
        @pl.when(tm == 1)
        def _():
            for f in range(2):
                copy_of(buf, phase, "mate", f).wait_recv()

    def wait_edges(buf, phase, f):
        @pl.when(has_up)
        def _():
            copy_of(buf, phase, "down", f).wait_recv()

        @pl.when(tm == 0)
        def _():
            copy_of(buf, phase, "mate_top", f).start()

        @pl.when(has_down)
        def _():
            copy_of(buf, phase, "up", f).wait_recv()

        @pl.when(tm == 0)
        def _():
            copy_of(buf, phase, "mate_bottom", f).start()

    def wait_mate_edges(buf, phase, f):
        @pl.when(tm == 1)
        def _():
            copy_of(buf, phase, "mate_top", f).wait_recv()
            copy_of(buf, phase, "mate_bottom", f).wait_recv()

    def wait_sends(buf, phase):
        got = stat_got.at[phase]
        pltpu.make_async_copy(got, got, send_sem.at[phase, 10]).wait()
        for f in range(2):

            @pl.when(has_up)
            def _():
                copy_of(buf, phase, "up", f).wait_send()

            @pl.when(has_down)
            def _():
                copy_of(buf, phase, "down", f).wait_send()

            @pl.when(tm == 0)
            def _():
                copy_of(buf, phase, "mate", f).wait_send()
                copy_of(buf, phase, "mate_top", f).wait_send()
                copy_of(buf, phase, "mate_bottom", f).wait_send()

    def normalized(values, mean, scale, shift):
        normed = (values - mean) * scale + shift
        return normed * (0.5 + 0.5 * jnp.tanh(0.5 * normed))

    row = lax.broadcasted_iota(jnp.int32, (cols, chans), 0)

    def put_taps(frame, slot, h):
        before = jnp.where(row == 0, 0.0, pltpu.roll(h, 1, 0))
        after = jnp.where(row == cols - 1, 0.0, pltpu.roll(h, cols - 1, 0))
        rows, base = pl.ds(frame * cols, cols), slot * 3 * chans
        taps[rows, base : base + chans] = before.astype(jnp.bfloat16)
        taps[rows, base + chans : base + 2 * chans] = h.astype(jnp.bfloat16)
        taps[rows, base + 2 * chans : base + 3 * chans] = after.astype(jnp.bfloat16)

    wide = 3 * chans
    none = jnp.zeros((wide, chans), jnp.bfloat16)

    def conv_part(weight, part, times):
        total = None
        for a in times:
            w = weight.at[a]
            if part == 0:
                kernel_a = jnp.concatenate([w[wide : 3 * wide], w[0 : 2 * wide]], axis=1)
            else:
                kernel_a = jnp.concatenate(
                    [
                        jnp.concatenate([w[0:wide], none], axis=0),
                        jnp.concatenate([none, w[2 * wide : 3 * wide]], axis=0),
                    ],
                    axis=1,
                )
            x = taps[a * cols : (a + 2) * cols, part * 2 * wide : (part + 1) * 2 * wide]
            y = jnp.dot(x, kernel_a, preferred_element_type=jnp.float32)
            total = y if total is None else total + y
        return total

    own = [(f, s) for f in (2, 3) for s in (0, 1)]
    past = [(f, s) for f in (0, 1) for s in (0, 1)]

    def source_frame(f):
        return jnp.where(tm == 0, 2, f) if f < 2 else f

    sums = jnp.zeros((1, chans), jnp.float32)
    squares = jnp.zeros((1, chans), jnp.float32)
    for f, s in own:
        values = raw[f, s].astype(jnp.float32)
        sums = sums + jnp.sum(values, axis=0, keepdims=True)
        squares = squares + jnp.sum(values * values, axis=0, keepdims=True)
    put_stats(0, sums, squares)
    pl.semaphore_wait(barrier, count - 1)
    send_stats(0)
    for f in range(2):
        send_edges(raw, 0, f)

    mean, scale = get_stats(0, gain_first[...])
    shift = shift_first[...]

    def first_hidden(f, s):
        h = normalized(raw[source_frame(f), s].astype(jnp.float32), mean, scale, shift)
        if s == 2:
            h = jnp.where(has_up, h, 0.0)
        if s == 3:
            h = jnp.where(has_down, h, 0.0)
        put_taps(f, s, h)

    for f, s in own:
        first_hidden(f, s)
    load_first.wait()
    first_out[...] = conv_part(weight_first, 0, (2,))
    wait_mate(raw, 0)
    for f, s in past:
        first_hidden(f, s)
    first_out[...] = first_out[...] + conv_part(weight_first, 0, (0, 1))
    for f in range(2):
        wait_edges(raw, 0, f)
    for f in range(2):
        for s in (2, 3):
            first_hidden(f + 2, s)
    first_out[...] = first_out[...] + conv_part(weight_first, 1, (2,))
    for f in range(2):
        wait_mate_edges(raw, 0, f)
        for s in (2, 3):
            first_hidden(f, s)
    first = first_out[...] + conv_part(weight_first, 1, (0, 1))
    first_out[...] = first

    sums = jnp.sum(first, axis=0, keepdims=True)
    squares = jnp.sum(first * first, axis=0, keepdims=True)
    put_stats(1, sums[:, :chans] + sums[:, chans:], squares[:, :chans] + squares[:, chans:])
    send_stats(1)
    mean, scale = get_stats(1, gain_second[...])
    shift = shift_second[...]
    for f, s in own:
        h = normalized(
            first_out[(f - 2) * cols : (f - 1) * cols, s * chans : (s + 1) * chans],
            mean,
            scale,
            shift,
        )
        hid[f, s] = h.astype(jnp.bfloat16)
        if s == 1:
            send_edges(hid, 1, f - 2)

    def second_hidden(f, s):
        put_taps(f, s, hid[source_frame(f), s].astype(jnp.float32))

    for f, s in own:
        second_hidden(f, s)
    load_second.wait()
    first_out[...] = conv_part(weight_second, 0, (2,))
    wait_mate(hid, 1)
    for f, s in past:
        second_hidden(f, s)
    first_out[...] = first_out[...] + conv_part(weight_second, 0, (0, 1))
    for f in range(2):
        wait_edges(hid, 1, f)
    for f in range(2):
        for s in (2, 3):
            second_hidden(f + 2, s)
    first_out[...] = first_out[...] + conv_part(weight_second, 1, (2,))
    for f in range(2):
        wait_mate_edges(hid, 1, f)
        for s in (2, 3):
            second_hidden(f, s)
    branch = first_out[...] + conv_part(weight_second, 1, (0, 1))
    bias = bias_second[...]
    stores = [
        pltpu.make_async_copy(result.at[f], out.at[f], local_sem.at[3 + f]) for f in range(2)
    ]
    for f, s in own:
        value = branch[(f - 2) * cols : (f - 1) * cols, s * chans : (s + 1) * chans]
        result[f - 2, s] = (raw[f, s].astype(jnp.float32) + value + bias).astype(jnp.bfloat16)
        if s == 1:
            stores[f - 2].start()
    wait_sends(raw, 0)
    wait_sends(hid, 1)
    for store in stores:
        store.wait()


def solution(mesh):
    tiles = mesh.shape["tile"]
    count = tiles * mesh.shape["tm"]

    def step(video, conv_first, conv_second, *vectors):
        frames, rows, cols, chans = video.shape
        any_spec = pl.BlockSpec(memory_space=pl.ANY)
        vmem_spec = pl.BlockSpec(memory_space=pltpu.VMEM)
        bf16, f32 = jnp.bfloat16, jnp.float32
        return pl.pallas_call(
            functools.partial(kernel, tiles),
            out_shape=jax.ShapeDtypeStruct(video.shape, bf16),
            in_specs=[any_spec] * 3 + [vmem_spec] * 5,
            out_specs=any_spec,
            scratch_shapes=[
                pltpu.VMEM((frames + 2, rows + 2, cols, chans), bf16),
                pltpu.VMEM((frames + 2, rows + 2, cols, chans), bf16),
                pltpu.VMEM(((frames + 2) * cols, (rows + 2) * 3 * chans), bf16),
                pltpu.VMEM((3, 9 * chans, chans), bf16),
                pltpu.VMEM((3, 9 * chans, chans), bf16),
                pltpu.VMEM((frames * cols, rows * chans), f32),
                pltpu.VMEM(video.shape, bf16),
                pltpu.VMEM((2, 8, chans), f32),
                pltpu.VMEM((2, count - 1, 8, chans), f32),
                pltpu.SemaphoreType.DMA((5,)),
                pltpu.SemaphoreType.DMA((2, 11)),
                pltpu.SemaphoreType.DMA((2, 11)),
            ],
            compiler_params=pltpu.CompilerParams(
                collective_id=0, has_side_effects=True, vmem_limit_bytes=62 * 1024 * 1024
            ),
        )(
            video,
            conv_first.reshape(3, 9 * chans, chans),
            conv_second.reshape(3, 9 * chans, chans),
            *[v.reshape(1, chans) for v in vectors],
        )

    block = P(("grp", "tm"), "tile", None, None)
    return jax.shard_map(
        step, mesh=mesh, in_specs=(block,) + (P(),) * 7, out_specs=block, check_vma=False
    )
```

```python
import functools

import jax
import jax.numpy as jnp
from jax import lax
from jax.experimental import pallas as pl
from jax.experimental.pallas import tpu as pltpu
from jax.sharding import PartitionSpec as P

G = 32
EPSILON = 1e-06
MESH = pl.DeviceIdType.MESH


def group_sums(x, width):
    lanes = x.shape[-1]
    lane = lax.broadcasted_iota(jnp.int32, x.shape, 1)
    step = 1
    while step < width:
        odd = (lane // step) % 2 == 1
        x = x + jnp.where(odd, pltpu.roll(x, step, 1), pltpu.roll(x, lanes - step, 1))
        step *= 2
    return x


def kernel(
    tiles,
    video,
    conv_first,
    conv_second,
    gain_first,
    shift_first,
    gain_second,
    shift_second,
    bias_second,
    out,
    raw,
    hid,
    taps,
    weight_first,
    weight_second,
    first_out,
    result,
    stat_mine,
    stat_got,
    local_sem,
    send_sem,
    recv_sem,
):
    count = tiles * 2
    tile, tm = lax.axis_index("tile"), lax.axis_index("tm")
    cols, chans = raw.shape[2], raw.shape[3]
    cells = float(count * 4 * cols * (chans // G))
    has_up, has_down = tile > 0, tile < tiles - 1

    load_video = pltpu.make_async_copy(video, raw.at[pl.ds(2, 2), pl.ds(0, 2)], local_sem.at[0])
    load_first = pltpu.make_async_copy(conv_first, weight_first, local_sem.at[1])
    load_second = pltpu.make_async_copy(conv_second, weight_second, local_sem.at[2])
    load_video.start()

    def peer(step, other_core):
        other = tile + step
        return {
            "tile": jnp.where(other >= tiles, other - tiles, other),
            "tm": 1 - tm if other_core else tm,
        }

    def each_peer(visit):
        visit(0, {"tile": tile, "tm": 1 - tm})
        for core in range(2):
            if tiles <= 8:
                for step in range(1, tiles):
                    visit(2 * step - 1 + core, peer(step, core))
            else:

                @pl.loop(1, tiles)
                def _(step):
                    visit(2 * step - 1 + core, peer(step, core))

    barrier = pltpu.get_barrier_semaphore()

    def greet(slot, device):
        pl.semaphore_signal(barrier, inc=1, device_id=device, device_id_type=MESH)

    each_peer(greet)
    load_first.start()
    load_second.start()

    @pl.when(jnp.logical_not(has_up))
    def _():
        raw[:, 2] = jnp.zeros((4, cols, chans), jnp.bfloat16)
        hid[:, 2] = jnp.zeros((4, cols, chans), jnp.bfloat16)

    @pl.when(jnp.logical_not(has_down))
    def _():
        raw[:, 3] = jnp.zeros((4, cols, chans), jnp.bfloat16)
        hid[:, 3] = jnp.zeros((4, cols, chans), jnp.bfloat16)

    load_video.wait()

    def put_stats(phase, sums, squares):
        row = lax.broadcasted_iota(jnp.int32, (8, chans), 0)
        stat_mine[phase] = jnp.where(row == 0, sums, jnp.where(row == 1, squares, 0.0))

    def send_stats(phase):
        def send(slot, device):
            pltpu.make_async_remote_copy(
                src_ref=stat_mine.at[phase],
                dst_ref=stat_got.at[phase, slot],
                send_sem=send_sem.at[phase, 10],
                recv_sem=recv_sem.at[phase, 10],
                device_id=device,
                device_id_type=MESH,
            ).start()

        each_peer(send)

    def get_stats(phase, gain):
        got = stat_got.at[phase]
        pltpu.make_async_copy(got, got, recv_sem.at[phase, 10]).wait()
        total = group_sums(stat_mine[phase] + jnp.sum(stat_got[phase], axis=0), chans // G)
        mean = total[0:1] / cells
        spread = total[1:2] / cells - mean * mean
        return mean, lax.rsqrt(spread + EPSILON) * (0.5 * gain)

    def copy_of(buf, phase, which, f):
        src, dst, device = {
            "up": (buf.at[2 + f, 0], buf.at[2 + f, 3], {"tile": tile - 1, "tm": tm}),
            "down": (buf.at[2 + f, 1], buf.at[2 + f, 2], {"tile": tile + 1, "tm": tm}),
            "mate": (
                buf.at[2 + f, pl.ds(0, 2)],
                buf.at[f, pl.ds(0, 2)],
                {"tile": tile, "tm": 1 - tm},
            ),
            "mate_top": (buf.at[2 + f, 2], buf.at[f, 2], {"tile": tile, "tm": 1 - tm}),
            "mate_bottom": (buf.at[2 + f, 3], buf.at[f, 3], {"tile": tile, "tm": 1 - tm}),
        }[which]
        at = ("up", "down", "mate", "mate_top", "mate_bottom").index(which) * 2 + f
        return pltpu.make_async_remote_copy(
            src_ref=src,
            dst_ref=dst,
            send_sem=send_sem.at[phase, at],
            recv_sem=recv_sem.at[phase, at],
            device_id=device,
            device_id_type=MESH,
        )

    def send_edges(buf, phase, f):
        @pl.when(has_up)
        def _():
            copy_of(buf, phase, "up", f).start()

        @pl.when(has_down)
        def _():
            copy_of(buf, phase, "down", f).start()

        @pl.when(tm == 0)
        def _():
            copy_of(buf, phase, "mate", f).start()

    def wait_mate(buf, phase):
        @pl.when(tm == 1)
        def _():
            for f in range(2):
                copy_of(buf, phase, "mate", f).wait_recv()

    def wait_edges(buf, phase, f):
        @pl.when(has_up)
        def _():
            copy_of(buf, phase, "down", f).wait_recv()

        @pl.when(tm == 0)
        def _():
            copy_of(buf, phase, "mate_top", f).start()

        @pl.when(has_down)
        def _():
            copy_of(buf, phase, "up", f).wait_recv()

        @pl.when(tm == 0)
        def _():
            copy_of(buf, phase, "mate_bottom", f).start()

    def wait_mate_edges(buf, phase, f):
        @pl.when(tm == 1)
        def _():
            copy_of(buf, phase, "mate_top", f).wait_recv()
            copy_of(buf, phase, "mate_bottom", f).wait_recv()

    def wait_sends(buf, phase):
        got = stat_got.at[phase]
        pltpu.make_async_copy(got, got, send_sem.at[phase, 10]).wait()
        for f in range(2):

            @pl.when(has_up)
            def _():
                copy_of(buf, phase, "up", f).wait_send()

            @pl.when(has_down)
            def _():
                copy_of(buf, phase, "down", f).wait_send()

            @pl.when(tm == 0)
            def _():
                copy_of(buf, phase, "mate", f).wait_send()
                copy_of(buf, phase, "mate_top", f).wait_send()
                copy_of(buf, phase, "mate_bottom", f).wait_send()

    def normalized(values, mean, scale, shift):
        half = (values - mean) * scale + shift
        return half + half * jnp.tanh(half)

    row = lax.broadcasted_iota(jnp.int32, (cols, chans), 0)

    def put_taps(frame, slot, h):
        before = jnp.where(row == 0, 0.0, pltpu.roll(h, 1, 0))
        after = jnp.where(row == cols - 1, 0.0, pltpu.roll(h, cols - 1, 0))
        rows, base = pl.ds(frame * cols, cols), slot * 3 * chans
        taps[rows, base : base + chans] = before.astype(jnp.bfloat16)
        taps[rows, base + chans : base + 2 * chans] = h.astype(jnp.bfloat16)
        taps[rows, base + 2 * chans : base + 3 * chans] = after.astype(jnp.bfloat16)

    wide = 3 * chans
    none = jnp.zeros((wide, chans), jnp.bfloat16)

    def conv_part(weight, part, times):
        total = None
        for a in times:
            w = weight.at[a]
            if part == 0:
                kernel_a = jnp.concatenate([w[wide : 3 * wide], w[0 : 2 * wide]], axis=1)
            else:
                kernel_a = jnp.concatenate(
                    [
                        jnp.concatenate([w[0:wide], none], axis=0),
                        jnp.concatenate([none, w[2 * wide : 3 * wide]], axis=0),
                    ],
                    axis=1,
                )
            x = taps[a * cols : (a + 2) * cols, part * 2 * wide : (part + 1) * 2 * wide]
            y = jnp.dot(x, kernel_a, preferred_element_type=jnp.float32)
            total = y if total is None else total + y
        return total

    own = [(f, s) for f in (2, 3) for s in (0, 1)]
    past = [(f, s) for f in (0, 1) for s in (0, 1)]

    def source_frame(f):
        return jnp.where(tm == 0, 2, f) if f < 2 else f

    sums = jnp.zeros((1, chans), jnp.float32)
    squares = jnp.zeros((1, chans), jnp.float32)
    for f, s in own:
        values = raw[f, s].astype(jnp.float32)
        sums = sums + jnp.sum(values, axis=0, keepdims=True)
        squares = squares + jnp.sum(values * values, axis=0, keepdims=True)
    put_stats(0, sums, squares)
    pl.semaphore_wait(barrier, count - 1)
    send_stats(0)
    for f in range(2):
        send_edges(raw, 0, f)

    mean, scale = get_stats(0, gain_first[...])
    shift = 0.5 * shift_first[...]

    def first_hidden(f, s):
        h = normalized(raw[source_frame(f), s].astype(jnp.float32), mean, scale, shift)
        if s == 2:
            h = jnp.where(has_up, h, 0.0)
        if s == 3:
            h = jnp.where(has_down, h, 0.0)
        put_taps(f, s, h)

    for f, s in own:
        first_hidden(f, s)
    load_first.wait()
    first_out[...] = conv_part(weight_first, 0, (2,))
    wait_mate(raw, 0)
    for f, s in past:
        first_hidden(f, s)
    first_out[...] = first_out[...] + conv_part(weight_first, 0, (0, 1))
    for f in range(2):
        wait_edges(raw, 0, f)
    for f in range(2):
        for s in (2, 3):
            first_hidden(f + 2, s)
    first_out[...] = first_out[...] + conv_part(weight_first, 1, (2,))
    for f in range(2):
        wait_mate_edges(raw, 0, f)
        for s in (2, 3):
            first_hidden(f, s)
    first = first_out[...] + conv_part(weight_first, 1, (0, 1))
    first_out[...] = first

    sums = jnp.sum(first, axis=0, keepdims=True)
    squares = jnp.sum(first * first, axis=0, keepdims=True)
    put_stats(1, sums[:, :chans] + sums[:, chans:], squares[:, :chans] + squares[:, chans:])
    send_stats(1)
    mean, scale = get_stats(1, gain_second[...])
    shift = 0.5 * shift_second[...]
    for f, s in own:
        h = normalized(
            first_out[(f - 2) * cols : (f - 1) * cols, s * chans : (s + 1) * chans],
            mean,
            scale,
            shift,
        )
        hid[f, s] = h.astype(jnp.bfloat16)
        if s == 1:
            send_edges(hid, 1, f - 2)

    def second_hidden(f, s):
        put_taps(f, s, hid[source_frame(f), s].astype(jnp.float32))

    for f, s in own:
        second_hidden(f, s)
    load_second.wait()
    first_out[...] = conv_part(weight_second, 0, (2,))
    wait_mate(hid, 1)
    for f, s in past:
        second_hidden(f, s)
    first_out[...] = first_out[...] + conv_part(weight_second, 0, (0, 1))
    for f in range(2):
        wait_edges(hid, 1, f)
    for f in range(2):
        for s in (2, 3):
            second_hidden(f + 2, s)
    first_out[...] = first_out[...] + conv_part(weight_second, 1, (2,))
    for f in range(2):
        wait_mate_edges(hid, 1, f)
        for s in (2, 3):
            second_hidden(f, s)
    branch = first_out[...] + conv_part(weight_second, 1, (0, 1))
    bias = bias_second[...]
    stores = [
        pltpu.make_async_copy(result.at[f], out.at[f], local_sem.at[3 + f]) for f in range(2)
    ]
    for f, s in own:
        value = branch[(f - 2) * cols : (f - 1) * cols, s * chans : (s + 1) * chans]
        result[f - 2, s] = (raw[f, s].astype(jnp.float32) + value + bias).astype(jnp.bfloat16)
        if s == 1:
            stores[f - 2].start()
    wait_sends(raw, 0)
    wait_sends(hid, 1)
    for store in stores:
        store.wait()


def solution(mesh):
    tiles = mesh.shape["tile"]
    count = tiles * mesh.shape["tm"]

    def step(video, conv_first, conv_second, *vectors):
        frames, rows, cols, chans = video.shape
        any_spec = pl.BlockSpec(memory_space=pl.ANY)
        vmem_spec = pl.BlockSpec(memory_space=pltpu.VMEM)
        bf16, f32 = jnp.bfloat16, jnp.float32
        return pl.pallas_call(
            functools.partial(kernel, tiles),
            out_shape=jax.ShapeDtypeStruct(video.shape, bf16),
            in_specs=[any_spec] * 3 + [vmem_spec] * 5,
            out_specs=any_spec,
            scratch_shapes=[
                pltpu.VMEM((frames + 2, rows + 2, cols, chans), bf16),
                pltpu.VMEM((frames + 2, rows + 2, cols, chans), bf16),
                pltpu.VMEM(((frames + 2) * cols, (rows + 2) * 3 * chans), bf16),
                pltpu.VMEM((3, 9 * chans, chans), bf16),
                pltpu.VMEM((3, 9 * chans, chans), bf16),
                pltpu.VMEM((frames * cols, rows * chans), f32),
                pltpu.VMEM(video.shape, bf16),
                pltpu.VMEM((2, 8, chans), f32),
                pltpu.VMEM((2, count - 1, 8, chans), f32),
                pltpu.SemaphoreType.DMA((5,)),
                pltpu.SemaphoreType.DMA((2, 11)),
                pltpu.SemaphoreType.DMA((2, 11)),
            ],
            compiler_params=pltpu.CompilerParams(
                collective_id=0, has_side_effects=True, vmem_limit_bytes=62 * 1024 * 1024
            ),
        )(
            video,
            conv_first.reshape(3, 9 * chans, chans),
            conv_second.reshape(3, 9 * chans, chans),
            *[v.reshape(1, chans) for v in vectors],
        )

    block = P(("grp", "tm"), "tile", None, None)
    return jax.shard_map(
        step, mesh=mesh, in_specs=(block,) + (P(),) * 7, out_specs=block, check_vma=False
    )
```
